512 devices in a mesh: dp: 32 (over y, x, core), mp: 16 (over z).
Axes of the slice: x: 4, y: 4, z: 16, core: 2. Of those that a mesh axis runs over, the one named last changes fastest.
Arguments:
- logged: bfloat16 [8192, 1024], P('dp'), may hold values from -6 to 6
- row_ids: int32 [768], P('dp'), may hold values from 0 to 255
- actions: int32 [768], replicated, may hold values from 0 to 17
- next_actions: int32 [768], replicated, may hold values from 0 to 17
- boot: int32 [16, 768], P('mp'), may hold values from 0 to 767
- dyn_in: bfloat16 [16, 1024, 8192], P('mp', None, 'dp'), may hold values from -0.1875 to 0.1875
- dyn_embed: bfloat16 [16, 18, 8192], P('mp', None, 'dp'), may hold values from -6 to 6
- dyn_out: bfloat16 [16, 8192, 1024], P('mp', 'dp'), may hold values from -0.0625 to 0.0625
- reward_head: bfloat16 [16, 1024], P('mp'), may hold values from -0.1875 to 0.1875
- critic_in: bfloat16 [16, 1024, 4096], P('mp', None, 'dp'), may hold values from -0.1875 to 0.1875
- critic_embed: bfloat16 [16, 18, 4096], P('mp', None, 'dp'), may hold values from -6 to 6
- critic_head: bfloat16 [16, 4096], P('mp', 'dp'), may hold values from -0.09375 to 0.09375
Outputs:
- grad_in: float32 [16, 1024, 4096], P('mp', None, 'dp')
- grad_embed: float32 [16, 18, 4096], P('mp', None, 'dp')
- grad_head: float32 [16, 4096], P('mp', 'dp')
- target: float32 [768], P('dp')
The draws below stay inside these ranges and needn't reach their ends.
Inputs may be any that keep to these rules, and one draw needn't show every extreme that they name: Row r of the rollout reads logged row (r // 24) * 256 + row_ids[r]. `boot`: indices into all 768 rollout rows, repeats allowed.
All inputs are finite; a program needn't handle non-finite values.
Results may differ from the reference program's by a relative error of at most 0.0029.
Values may be sent and summed in bfloat16 or wider, within the bound.
A program may use at most 64 MiB of HBM per device.

```python
import jax
import jax.numpy as jnp
from jax import lax

D = 1024
HD = 8192
HC = 4096
NA = 18
ROWS_DEV = 24
LOG_DEV = 256
MEMBERS = 16
ROWS = 768
BOOT = 768
LOGGED = 8192


def place_ends(values, own_key, least, top_value):
    spot = [jax.random.randint(jax.random.fold_in(own_key, axis), (), 0, length) for axis, length in enumerate(values.shape)]
    longest = values.shape.index(max(values.shape))
    next_to = spot[:longest] + [(spot[longest] + 1) % values.shape[longest]] + spot[longest + 1:]
    return values.at[tuple(spot)].set(least).at[tuple(next_to)].set(top_value)


def shard_levels(rng, shape, pieces, least, top_value):
    def one(position, shards_of):
        heights = jax.random.uniform(jax.random.fold_in(jax.random.fold_in(rng, 6), position), (shards_of,), jnp.float32, least / len(pieces), top_value / len(pieces))
        return jnp.repeat(jnp.exp(heights), shape[position] // shards_of).reshape((-1,) + (1,) * (len(shape) - position - 1))

    gain = one(*pieces[0])
    for cut in pieces[1:]:
        gain = gain * one(*cut)
    return gain


def centred(stream_key, shape, spread, most, split=(), kind=jnp.bfloat16):
    level = shard_levels(stream_key, shape, split, -0.22, 0.18) if split else 1.0
    result = jax.random.normal(stream_key, shape, jnp.float32) * spread * level
    return jnp.minimum(jnp.maximum(result, -most), most).astype(kind)


def setup_inputs(seed: int = 0) -> dict:
    key_of = jax.random.split(jax.random.key(seed), 13)
    return {
        "logged": centred(key_of[0], (LOGGED, D), 1.0, 6.0, ((0, 32),)),
        "row_ids": place_ends(jax.random.randint(key_of[1], (ROWS,), 0, LOG_DEV), jax.random.fold_in(key_of[1], 1), 0, LOG_DEV - 1).astype(jnp.int32),
        "actions": place_ends(jax.random.randint(key_of[2], (ROWS,), 0, NA), jax.random.fold_in(key_of[2], 1), 0, NA - 1).astype(jnp.int32),
        "next_actions": place_ends(jax.random.randint(key_of[3], (ROWS,), 0, NA), jax.random.fold_in(key_of[3], 1), 0, NA - 1).astype(jnp.int32),
        "boot": place_ends(jax.random.randint(key_of[4], (MEMBERS, BOOT), 0, ROWS), jax.random.fold_in(key_of[4], 1), 0, ROWS - 1).astype(jnp.int32),
        "dyn_in": centred(key_of[5], (MEMBERS, D, HD), D ** -0.5, 0.1875, ((0, 16), (2, 32))),
        "dyn_embed": centred(key_of[6], (MEMBERS, NA, HD), 1.0, 6.0, ((0, 16), (2, 32))),
        "dyn_out": centred(key_of[7], (MEMBERS, HD, D), HD ** -0.5, 0.0625, ((0, 16), (1, 32))),
        "reward_head": centred(key_of[8], (MEMBERS, D), D ** -0.5, 0.1875, ((0, 16),)),
        "critic_in": centred(key_of[9], (MEMBERS, D, HC), D ** -0.5, 0.1875, ((0, 16), (2, 32))),
        "critic_embed": centred(key_of[10], (MEMBERS, NA, HC), 1.0, 6.0, ((0, 16), (2, 32))),
        "critic_head": centred(key_of[11], (MEMBERS, HC), HC ** -0.5, 0.09375, ((0, 16), (1, 32))),
    }


discount = 0.99
penalty_weight = 1.0

def silu_grad(preact):
    sigma_val = jax.nn.sigmoid(preact)
    return sigma_val * (1.0 + preact * (1.0 - sigma_val))

def reference(logged, row_ids, actions, next_actions, boot, dyn_in, dyn_embed, dyn_out, reward_head, critic_in, critic_embed, critic_head):
    block_of = jnp.arange(ROWS, dtype=jnp.int32) // ROWS_DEV
    states = logged[(block_of * LOG_DEV + row_ids).astype(jnp.int32)]
    act_hot = jax.nn.one_hot(actions, NA, dtype=jnp.bfloat16)
    next_hot = jax.nn.one_hot(next_actions, NA, dtype=jnp.bfloat16)

    def member_target(weights):
        w_in, w_embed, w_out, w_reward, c_in, c_embed, c_head = weights
        preact = jnp.dot(states, w_in, preferred_element_type=jnp.float32) + jnp.dot(act_hot, w_embed, preferred_element_type=jnp.float32)
        hidden = jax.nn.silu(preact).astype(jnp.bfloat16)
        increment = jnp.dot(hidden, w_out, preferred_element_type=jnp.float32)
        next_state = (states.astype(jnp.float32) + increment).astype(jnp.bfloat16)
        reward = jnp.dot(next_state, w_reward[:, None], preferred_element_type=jnp.float32)[:, 0]
        critic_pre = jnp.dot(next_state, c_in, preferred_element_type=jnp.float32) + jnp.dot(next_hot, c_embed, preferred_element_type=jnp.float32)
        value = lax.optimization_barrier(jnp.sum(jax.nn.silu(critic_pre) * c_head.astype(jnp.float32)[None, :], axis=1))
        return reward + discount * value
    bellman = lax.map(member_target, (dyn_in, dyn_embed, dyn_out, reward_head, critic_in, critic_embed, critic_head))
    mean_val = lax.optimization_barrier(jnp.sum(bellman, axis=0)) / MEMBERS
    spread_val = lax.optimization_barrier(jnp.sum(bellman * bellman, axis=0)) / MEMBERS - mean_val * mean_val
    target = mean_val - penalty_weight * jnp.sqrt(spread_val + 1.0)

    def member_td(inputs):
        picks, c_in, c_embed, c_head = inputs
        boot_states = states[picks]
        boot_hot = act_hot[picks]
        preact = jnp.dot(boot_states, c_in, preferred_element_type=jnp.float32) + jnp.dot(boot_hot, c_embed, preferred_element_type=jnp.float32)
        activ = jax.nn.silu(preact)
        head_wide = c_head.astype(jnp.float32)[None, :]
        q_value = lax.optimization_barrier(jnp.sum(activ * head_wide, axis=1))
        residual = q_value - target[picks]
        grad_h = lax.optimization_barrier(jnp.sum(residual[:, None] * activ, axis=0))
        back = (residual[:, None] * head_wide * silu_grad(preact)).astype(jnp.bfloat16)
        grad_w = lax.dot_general(boot_states, back, (((0,), (0,)), ((), ())), preferred_element_type=jnp.float32)
        grad_e = lax.dot_general(boot_hot, back, (((0,), (0,)), ((), ())), preferred_element_type=jnp.float32)
        return (grad_w, grad_e, grad_h)
    grad_in, grad_embed, grad_head = lax.map(member_td, (boot, critic_in, critic_embed, critic_head))
    return (grad_in, grad_embed, grad_head, target)
```

```python
import jax
import jax.numpy as jnp
from jax import lax
from jax.experimental import pallas as pl
from jax.experimental.pallas import tpu as pltpu
from jax.sharding import PartitionSpec as P

MESH = pl.DeviceIdType.MESH
F32 = jnp.float32
BF16 = jnp.bfloat16

discount = 0.99
penalty_weight = 1.0

CHUNKS = 3
CHIPS = 16
SIDE = 4
MEMBERS = 16
WIDTH = 1024
HALF = 512
LANES = 128
ACTS = 32


def nt(lhs, rhs):
    return lax.dot_general(lhs, rhs, (((1,), (1,)), ((), ())), preferred_element_type=F32)


def tn(lhs, rhs):
    return lax.dot_general(lhs, rhs, (((0,), (0,)), ((), ())), preferred_element_type=F32)


def nn(lhs, rhs):
    return jnp.dot(lhs, rhs, preferred_element_type=F32)


def sigmoid(v):
    return 0.5 * jnp.tanh(0.5 * v) + 0.5


def fold(block):
    return jnp.concatenate([block[:, :HALF], block[:, HALF:]], axis=0)


def unfold(block):
    return jnp.concatenate([block[:8], block[8:]], axis=1)


def iota(shape, dim):
    return lax.broadcasted_iota(jnp.int32, shape, dim)


def kernel(
    rowid_ref,
    act_ref,
    nact_ref,
    boot_ref,
    rhead_ref,
    chead_ref,
    demb_ref,
    cemb_ref,
    logged_hbm,
    din_hbm,
    dout_hbm,
    cin_hbm,
    gin_ref,
    gemb_ref,
    ghead_ref,
    tgt_ref,
    logv,
    wi,
    wo,
    wc,
    em,
    ce,
    hd,
    ag1,
    xs,
    ep,
    rss,
    rsr,
    ag2,
    wct,
    ecn,
    ecb,
    at,
    gt,
    xt,
    bt,
    acts,
    cnt,
    qv,
    ph6,
    zb,
    fin,
    loc_sem,
    wsend,
    wrecv,
    a_send,
    a_recv,
    r_send,
    r_recv,
    n_send,
    n_recv,
    x_send,
    x_recv,
    s_send,
    s_recv,
):
    dp = lax.axis_index("dp")
    zi = lax.axis_index("mp")
    core = dp % 2
    me = dp // 2
    px = me % SIDE
    py = me // SIDE
    sib = (dp + 1 - 2 * core, zi)

    def peer(step):
        chip = ((py + step // SIDE) % SIDE) * SIDE + (px + step % SIDE) % SIDE
        return chip, (chip * 2 + core, zi)

    loads = [
        pltpu.make_async_copy(logged_hbm, logv, loc_sem.at[0]),
        pltpu.make_async_copy(din_hbm, wi.at[0], loc_sem.at[1]),
        pltpu.make_async_copy(dout_hbm, wo.at[0], loc_sem.at[2]),
        pltpu.make_async_copy(cin_hbm, wc.at[0], loc_sem.at[3]),
    ]
    for load in loads:
        load.start()

    barrier = pltpu.get_barrier_semaphore()

    def greet_z(step, carry):
        pl.semaphore_signal(barrier, inc=1, device_id=(dp, (zi + step) % MEMBERS), device_id_type=MESH)
        return carry

    lax.fori_loop(1, MEMBERS, greet_z, 0)

    def greet(step, carry):
        pl.semaphore_signal(barrier, inc=1, device_id=peer(step)[1], device_id_type=MESH)
        return carry

    lax.fori_loop(1, CHIPS, greet, 0)
    pl.semaphore_signal(barrier, inc=1, device_id=sib, device_id_type=MESH)

    em[0] = nn((iota((ACTS, 18), 0) == iota((ACTS, 18), 1)).astype(BF16), demb_ref[...]).astype(BF16)
    ce[0] = nn((iota((ACTS, 18), 0) == iota((ACTS, 18), 1)).astype(BF16), cemb_ref[...]).astype(BF16)
    hd[0] = jnp.broadcast_to(chead_ref[...].astype(F32), (8, LANES))
    loads[0].wait()
    hot = (iota((256, 24), 0) == rowid_ref[...]).astype(BF16)
    picked = tn(hot, logv[...])
    for ch in range(CHUNKS):
        ag1[ch, me] = fold(picked[ch * 8 : ch * 8 + 8]).astype(BF16)

    pl.semaphore_wait(barrier, 2 * (CHIPS - 1) + 1)

    for ch in range(CHUNKS):

        def send_states(step, carry, ch=ch):
            pltpu.make_async_remote_copy(
                src_ref=ag1.at[ch, me],
                dst_ref=ag1.at[ch, me],
                send_sem=a_send.at[ch],
                recv_sem=a_recv.at[ch],
                device_id=peer(step)[1],
                device_id_type=MESH,
            ).start()
            return carry

        lax.fori_loop(1, CHIPS, send_states, 0)

    swaps = []
    for i, (src, dst) in enumerate(
        [
            (din_hbm, wi.at[1]),
            (em.at[0], em.at[1]),
            (dout_hbm, wo.at[1]),
            (cin_hbm, wc.at[1]),
            (ce.at[0], ce.at[1]),
            (hd.at[0], hd.at[1]),
        ]
    ):
        swaps.append(
            pltpu.make_async_remote_copy(
                src_ref=src,
                dst_ref=dst,
                send_sem=wsend.at[i],
                recv_sem=wrecv.at[i],
                device_id=sib,
                device_id_type=MESH,
            )
        )
        swaps[-1].start()

    lane = iota((1, LANES), 1)
    base = 48 * (lane // 8) + lane % 8
    stacked = jnp.concatenate(
        [act_ref[...].astype(F32), nact_ref[...].astype(F32), jnp.zeros((6, 768), F32)], axis=0
    ).astype(BF16)
    for half in range(2):
        who = core if half == 0 else 1 - core
        for ch in range(CHUNKS):
            rows = base + 24 * who + 8 * ch
            pick = (iota((768, LANES), 0) == rows).astype(BF16)
            acts[half * CHUNKS + ch] = nn(stacked, pick)
            total = jnp.zeros((LANES, LANES), F32)
            for part in range(6):
                column = jnp.broadcast_to(
                    boot_ref[:, part * LANES : (part + 1) * LANES].astype(F32), (LANES, LANES)
                ).T
                total = total + (column == rows.astype(F32)).astype(F32)
            cnt[half * CHUNKS + ch] = jnp.broadcast_to(jnp.sum(total, axis=0, keepdims=True), (8, LANES))

    def hot_t(slot, row):
        return (iota((ACTS, LANES), 0).astype(F32) == acts[slot][row : row + 1]).astype(BF16)

    for load in loads[1:]:
        load.wait()
    swaps[0].wait_recv()
    swaps[1].wait_recv()
    for ch in range(CHUNKS):
        hot_rows = hot_t(ch, 0)
        for s in range(2):
            ep[ch, s] = tn(hot_rows, em[s])
    swaps[2].wait_recv()

    def dynamics(ch, carry):
        slots = ag1.at[ch, pl.ds(0, CHIPS - 1)]
        pltpu.make_async_copy(slots, slots, a_recv.at[ch]).wait()
        x = jnp.concatenate([unfold(ag1[ch, j].astype(F32)) for j in range(CHIPS)], axis=0).astype(BF16)
        xs[0, ch] = x
        pltpu.make_async_remote_copy(
            src_ref=xs.at[0, ch],
            dst_ref=xs.at[1, ch],
            send_sem=x_send.at[ch],
            recv_sem=x_recv.at[ch],
            device_id=sib,
            device_id_type=MESH,
        ).start()
        inc = jnp.zeros((LANES, WIDTH), F32)
        for s in range(2):
            pre = nn(x, wi[s]) + ep[ch, s]
            inc = inc + nn((pre * sigmoid(pre)).astype(BF16), wo[s])
        for j in range(CHIPS):
            rss[ch, j] = fold(inc[j * 8 : j * 8 + 8]).astype(BF16)
        rsr[ch, me] = rss[ch, me]

        def send_sums(step, carry):
            chip, where = peer(step)
            pltpu.make_async_remote_copy(
                src_ref=rss.at[ch, chip],
                dst_ref=rsr.at[ch, me],
                send_sem=r_send.at[ch],
                recv_sem=r_recv.at[ch],
                device_id=where,
                device_id_type=MESH,
            ).start()
            return carry

        lax.fori_loop(1, CHIPS, send_sums, 0)
        return carry

    lax.fori_loop(0, CHUNKS, dynamics, 0)

    for i in range(3, 6):
        swaps[i].wait_recv()
    for s in range(2):
        wct[s * LANES : (s + 1) * LANES] = wc[s].T
    wct[256:272] = jnp.concatenate([rhead_ref[...].astype(F32), jnp.zeros((15, WIDTH), F32)], axis=0).astype(BF16)
    heads = [jnp.broadcast_to(hd[s][:1], (LANES, LANES)).T for s in range(2)]
    for ch in range(CHUNKS):
        for s in range(2):
            ecn[ch, s] = tn(ce[s], hot_t(ch, 1))
            ecb[ch, s] = tn(ce[s], hot_t(ch, 0))
        ecb[CHUNKS + ch, 0] = tn(ce[0], hot_t(CHUNKS + ch, 0))

    def own_units(slot, pre):
        gate = sigmoid(pre)
        act = pre * gate
        at[slot] = act
        gt[slot] = heads[0] * (gate * (1.0 + pre * (1.0 - gate)))
        return act

    for ch in range(CHUNKS):
        x = xs[0, ch]
        pre = nt(wct[:256], x)
        act0 = own_units(ch, pre[:LANES] + ecb[ch, 0])
        pre1 = pre[LANES:] + ecb[ch, 1]
        weighted = act0 * heads[0] + pre1 * sigmoid(pre1) * heads[1]
        qv[ch : ch + 1] = jnp.sum(weighted, axis=0, keepdims=True)
        xt[:, ch * LANES : (ch + 1) * LANES] = x.T

    def finish_rows(ch, carry):
        slots = rsr.at[ch, pl.ds(0, CHIPS - 1)]
        pltpu.make_async_copy(slots, slots, r_recv.at[ch]).wait()
        total = rsr[ch, 0].astype(F32)
        for j in range(1, CHIPS):
            total = total + rsr[ch, j].astype(F32)
        ag2[ch, me] = (ag1[ch, me].astype(F32) + total).astype(BF16)

        def send_next(step, carry):
            pltpu.make_async_remote_copy(
                src_ref=ag2.at[ch, me],
                dst_ref=ag2.at[ch, me],
                send_sem=n_send.at[ch],
                recv_sem=n_recv.at[ch],
                device_id=peer(step)[1],
                device_id_type=MESH,
            ).start()
            return carry

        lax.fori_loop(1, CHIPS, send_next, 0)
        return carry

    lax.fori_loop(0, CHUNKS, finish_rows, 0)

    for ch in range(CHUNKS):
        pltpu.make_async_copy(xs.at[1, ch], xs.at[1, ch], x_recv.at[ch]).wait()
        x = xs[1, ch]
        own_units(CHUNKS + ch, nt(wct[:LANES], x) + ecb[CHUNKS + ch, 0])
        xt[:, (CHUNKS + ch) * LANES : (CHUNKS + ch + 1) * LANES] = x.T

    rewards = []
    for ch in range(CHUNKS):
        slots = ag2.at[ch, pl.ds(0, CHIPS - 1)]
        pltpu.make_async_copy(slots, slots, n_recv.at[ch]).wait()
        x = jnp.concatenate([unfold(ag2[ch, j].astype(F32)) for j in range(CHIPS)], axis=0).astype(BF16)
        pre = nt(wct[...], x)
        pre0 = pre[:LANES] + ecn[ch, 0]
        pre1 = pre[LANES:256] + ecn[ch, 1]
        weighted = pre0 * sigmoid(pre0) * heads[0] + pre1 * sigmoid(pre1) * heads[1]
        ph6[me, ch : ch + 1] = jnp.sum(weighted, axis=0, keepdims=True)
        rewards.append(pre[256:257])
    ph6[me, 3:6] = qv[0:3]
    ph6[me, 6:8] = jnp.zeros((2, LANES), F32)

    far = [t ^ 10 for t in range(CHIPS) if t != 10]
    for step in far:
        pltpu.make_async_remote_copy(
            src_ref=ph6.at[me],
            dst_ref=ph6.at[me],
            send_sem=s_send.at[0],
            recv_sem=s_recv.at[0],
            device_id=peer(step)[1],
            device_id_type=MESH,
        ).start()
    slots = ph6.at[pl.ds(0, CHIPS - 1)]
    pltpu.make_async_copy(slots, slots, s_recv.at[0]).wait()
    sums = ph6[0]
    for j in range(1, CHIPS):
        sums = sums + ph6[j]
    reward = jnp.concatenate(rewards + [jnp.zeros((5, LANES), F32)], axis=0)
    zb[zi] = reward + discount * sums
    for step in (8, 7, 9, 6, 10, 5, 11, 4, 12, 3, 13, 2, 14, 1, 15):
        pltpu.make_async_remote_copy(
            src_ref=zb.at[zi],
            dst_ref=zb.at[zi],
            send_sem=s_send.at[1],
            recv_sem=s_recv.at[1],
            device_id=(dp, (zi + step) % MEMBERS),
            device_id_type=MESH,
        ).start()
    slots = zb.at[pl.ds(0, MEMBERS - 1)]
    pltpu.make_async_copy(slots, slots, s_recv.at[1]).wait()
    total = zb[0]
    square = total * total
    for m in range(1, MEMBERS):
        one = zb[m]
        total = total + one
        square = square + one * one
    mean = total / MEMBERS
    spread = square / MEMBERS - mean * mean
    target = mean - penalty_weight * jnp.sqrt(spread + 1.0)
    fin[0] = jnp.concatenate([target[:3], sums[3:6], jnp.zeros((2, LANES), F32)], axis=0)
    last = pltpu.make_async_remote_copy(
        src_ref=fin.at[0],
        dst_ref=fin.at[1],
        send_sem=s_send.at[2],
        recv_sem=s_recv.at[2],
        device_id=sib,
        device_id_type=MESH,
    )
    last.start()

    turned = pltpu.roll(target, (LANES - 8 * me) % LANES, 1)
    line = turned[0:1]
    for ch in range(1, CHUNKS):
        line = jnp.where(lane // 8 == ch, pltpu.roll(turned, 8 * ch, 1)[ch : ch + 1], line)
    tgt_ref[...] = line[:, :24]

    head_sum = jnp.zeros((LANES, LANES), F32)
    for half in range(2):
        if half == 1:
            last.wait_recv()
        ends = fin[half]
        for ch in range(CHUNKS):
            slot = half * CHUNKS + ch
            scaled = cnt[slot][:1] * (ends[3 + ch : 4 + ch] - ends[ch : ch + 1])
            head_sum = head_sum + scaled * at[slot]
            bt[:, slot * LANES : (slot + 1) * LANES] = (scaled * gt[slot]).astype(BF16)
    back = bt[...]
    gin_ref[...] = nt(xt[...], back)
    hots = jnp.concatenate([hot_t(slot, 0) for slot in range(2 * CHUNKS)], axis=1)
    gemb_ref[...] = nt(hots, back)[:18]
    ghead_ref[...] = jnp.sum(head_sum.T, axis=0, keepdims=True)

    last.wait_send()
    for swap in swaps:
        swap.wait_send()

    def drain(ch, carry):
        for buf, sem in ((ag1, a_send), (rss, r_send), (ag2, n_send)):
            slots = buf.at[ch, pl.ds(0, CHIPS - 1)]
            pltpu.make_async_copy(slots, slots, sem.at[ch]).wait()
        pltpu.make_async_copy(xs.at[0, ch], xs.at[0, ch], x_send.at[ch]).wait()
        return carry

    lax.fori_loop(0, CHUNKS, drain, 0)
    for i, buf in enumerate((ph6, zb)):
        slots = buf.at[pl.ds(0, CHIPS - 1)]
        pltpu.make_async_copy(slots, slots, s_send.at[i]).wait()


def local(
    logged,
    row_ids,
    actions,
    next_actions,
    boot,
    dyn_in,
    dyn_embed,
    dyn_out,
    reward_head,
    critic_in,
    critic_embed,
    critic_head,
):
    vmem = pl.BlockSpec(memory_space=pltpu.VMEM)
    hbm = pl.BlockSpec(memory_space=pl.ANY)
    dma = pltpu.SemaphoreType.DMA
    blocks = (CHUNKS, CHIPS, 16, HALF)
    grad_in, grad_embed, grad_head, target = pl.pallas_call(
        kernel,
        out_shape=(
            jax.ShapeDtypeStruct((WIDTH, LANES), F32),
            jax.ShapeDtypeStruct((18, LANES), F32),
            jax.ShapeDtypeStruct((1, LANES), F32),
            jax.ShapeDtypeStruct((1, 24), F32),
        ),
        in_specs=[vmem] * 8 + [hbm] * 4,
        out_specs=(vmem,) * 4,
        scratch_shapes=[
            pltpu.VMEM((256, WIDTH), BF16),
            pltpu.VMEM((2, WIDTH, 256), BF16),
            pltpu.VMEM((2, 256, WIDTH), BF16),
            pltpu.VMEM((2, WIDTH, LANES), BF16),
            pltpu.VMEM((2, ACTS, 256), BF16),
            pltpu.VMEM((2, ACTS, LANES), BF16),
            pltpu.VMEM((2, 8, LANES), F32),
            pltpu.VMEM(blocks, BF16),
            pltpu.VMEM((2, CHUNKS, LANES, WIDTH), BF16),
            pltpu.VMEM((CHUNKS, 2, LANES, 256), F32),
            pltpu.VMEM(blocks, BF16),
            pltpu.VMEM(blocks, BF16),
            pltpu.VMEM(blocks, BF16),
            pltpu.VMEM((272, WIDTH), BF16),
            pltpu.VMEM((CHUNKS, 2, LANES, LANES), F32),
            pltpu.VMEM((2 * CHUNKS, 2, LANES, LANES), F32),
            pltpu.VMEM((2 * CHUNKS, LANES, LANES), F32),
            pltpu.VMEM((2 * CHUNKS, LANES, LANES), F32),
            pltpu.VMEM((WIDTH, 768), BF16),
            pltpu.VMEM((LANES, 768), BF16),
            pltpu.VMEM((2 * CHUNKS, 8, LANES), F32),
            pltpu.VMEM((2 * CHUNKS, 8, LANES), F32),
            pltpu.VMEM((8, LANES), F32),
            pltpu.VMEM((CHIPS, 8, LANES), F32),
            pltpu.VMEM((MEMBERS, 8, LANES), F32),
            pltpu.VMEM((2, 8, LANES), F32),
            dma((4,)),
            dma((6,)),
            dma((6,)),
            dma((CHUNKS,)),
            dma((CHUNKS,)),
            dma((CHUNKS,)),
            dma((CHUNKS,)),
            dma((CHUNKS,)),
            dma((CHUNKS,)),
            dma((CHUNKS,)),
            dma((CHUNKS,)),
            dma((3,)),
            dma((3,)),
        ],
        compiler_params=pltpu.CompilerParams(
            collective_id=0, has_side_effects=True, vmem_limit_bytes=48 * 2**20
        ),
        name="rollout",
    )(
        row_ids[None],
        actions[None],
        next_actions[None],
        boot,
        reward_head,
        critic_head,
        dyn_embed[0],
        critic_embed[0],
        logged,
        dyn_in[0],
        dyn_out[0],
        critic_in[0],
    )
    return grad_in[None], grad_embed[None], grad_head, target[0]


def solution(mesh):
    return jax.shard_map(
        local,
        mesh=mesh,
        in_specs=(
            P("dp", None),
            P("dp"),
            P(),
            P(),
            P("mp", None),
            P("mp", None, "dp"),
            P("mp", None, "dp"),
            P("mp", "dp", None),
            P("mp", None),
            P("mp", None, "dp"),
            P("mp", None, "dp"),
            P("mp", "dp"),
        ),
        out_specs=(P("mp", None, "dp"), P("mp", None, "dp"), P("mp", "dp"), P("dp")),
        check_vma=False,
    )
```

```python
import jax
import jax.numpy as jnp
from jax import lax
from jax.experimental import pallas as pl
from jax.experimental.pallas import tpu as pltpu
from jax.sharding import PartitionSpec as P

MESH = pl.DeviceIdType.MESH
F32 = jnp.float32
BF16 = jnp.bfloat16

discount = 0.99
penalty_weight = 1.0

CHUNKS = 3
CHIPS = 16
SIDE = 4
MEMBERS = 16
WIDTH = 1024
HALF = 512
LANES = 128
ACTS = 32

AG1_GROUP = 1
RS_GROUP = 1
AG2_GROUP = 1

HOPS = (0, 1, 2, 1)
PLANE_ORDER = sorted(
    [(other, step) for other in range(2) for step in range(CHIPS) if other or step],
    key=lambda pair: (-HOPS[pair[1] // SIDE] - HOPS[pair[1] % SIDE], pair),
)
Z_ORDER = (8, 7, 9, 6, 10, 5, 11, 4, 12, 3, 13, 2, 14, 1, 15)


def nt(lhs, rhs):
    return lax.dot_general(lhs, rhs, (((1,), (1,)), ((), ())), preferred_element_type=F32)


def tn(lhs, rhs):
    return lax.dot_general(lhs, rhs, (((0,), (0,)), ((), ())), preferred_element_type=F32)


def nn(lhs, rhs):
    return jnp.dot(lhs, rhs, preferred_element_type=F32)


def sigmoid(v):
    return 0.5 * jnp.tanh(0.5 * v) + 0.5


def fold(block):
    return jnp.concatenate([block[:, :HALF], block[:, HALF:]], axis=0)


def unfold(block):
    return jnp.concatenate([block[:8], block[8:]], axis=1)


def iota(shape, dim):
    return lax.broadcasted_iota(jnp.int32, shape, dim)


def kernel(
    rowid_hbm,
    act_hbm,
    nact_hbm,
    boot_hbm,
    rhead_hbm,
    chead_hbm,
    demb_hbm,
    cemb_hbm,
    logged_hbm,
    din_hbm,
    dout_hbm,
    cin_hbm,
    gin_ref,
    gemb_ref,
    ghead_ref,
    tgt_ref,
    rowid_ref,
    act_ref,
    nact_ref,
    boot_ref,
    rhead_ref,
    chead_ref,
    demb_ref,
    cemb_ref,
    logv,
    wi,
    wo,
    wc,
    em,
    ce,
    hd,
    ag1,
    xs,
    ep,
    rss,
    rsr,
    ag2,
    wct,
    ecn,
    ecb,
    at,
    gt,
    xt,
    bt,
    acts,
    cnt,
    qv,
    ph6,
    zb,
    loc_sem,
    wsend,
    wrecv,
    a_send,
    a_recv,
    r_send,
    r_recv,
    n_send,
    n_recv,
    x_send,
    x_recv,
    s_send,
    s_recv,
):
    dp = lax.axis_index("dp")
    zi = lax.axis_index("mp")
    core = dp % 2
    me = dp // 2
    px = me % SIDE
    py = me // SIDE
    sib = (dp + 1 - 2 * core, zi)

    def peer(step, other=0):
        chip = ((py + step // SIDE) % SIDE) * SIDE + (px + step % SIDE) % SIDE
        return chip, (chip * 2 + (core + other) % 2, zi)

    loads = [
        pltpu.make_async_copy(src, dst, loc_sem.at[i])
        for i, (src, dst) in enumerate(
            [
                (logged_hbm, logv),
                (rowid_hbm, rowid_ref),
                (demb_hbm, demb_ref),
                (cemb_hbm, cemb_ref),
                (chead_hbm, chead_ref),
                (act_hbm, act_ref),
                (nact_hbm, nact_ref),
                (boot_hbm, boot_ref),
                (rhead_hbm, rhead_ref),
                (din_hbm, wi.at[0]),
                (dout_hbm, wo.at[0]),
                (cin_hbm, wc.at[0]),
            ]
        )
    ]
    for load in loads[:2]:
        load.start()

    barrier = pltpu.get_barrier_semaphore()
    for step in Z_ORDER:
        pl.semaphore_signal(barrier, inc=1, device_id=(dp, (zi + step) % MEMBERS), device_id_type=MESH)
    for other, step in PLANE_ORDER:
        pl.semaphore_signal(barrier, inc=1, device_id=peer(step, other)[1], device_id_type=MESH)
    for load in loads[2:]:
        load.start()

    loads[0].wait()
    loads[1].wait()
    hot = (iota((256, 24), 0) == rowid_ref[...].reshape(1, 24)).astype(BF16)
    picked = tn(hot, logv[...])
    for ch in range(CHUNKS):
        ag1[me, ch] = fold(picked[ch * 8 : ch * 8 + 8]).astype(BF16)
    pl.semaphore_wait(barrier, 31 + MEMBERS - 1)

    def spread(src, dst, send_sem, recv_sem, first, count):
        def one(step):
            chip, where = peer(step)
            pltpu.make_async_remote_copy(
                src_ref=src(chip).at[pl.ds(first, count)],
                dst_ref=dst.at[me, pl.ds(first, count)],
                send_sem=send_sem.at[first],
                recv_sem=recv_sem.at[first],
                device_id=where,
                device_id_type=MESH,
            ).start()

        for other, step in PLANE_ORDER:
            if other == 0:
                one(step)

    def landed(buf, sem, first, count):
        slots = buf.at[pl.ds(0, CHIPS - 1), pl.ds(first, count)]
        pltpu.make_async_copy(slots, slots, sem.at[first]).wait()

    for first in range(0, CHUNKS, AG1_GROUP):
        spread(lambda chip: ag1.at[me], ag1, a_send, a_recv, first, AG1_GROUP)

    for load in loads[2:]:
        load.wait()
    eye = (iota((ACTS, 18), 0) == iota((ACTS, 18), 1)).astype(BF16)
    em[0] = nn(eye, demb_ref[...]).astype(BF16)
    ce[0] = nn(eye, cemb_ref[...]).astype(BF16)
    hd[0] = jnp.broadcast_to(chead_ref[...].astype(F32), (8, LANES))

    swaps = []
    for i, (src, dst) in enumerate(
        [
            (din_hbm, wi.at[1]),
            (em.at[0], em.at[1]),
            (dout_hbm, wo.at[1]),
            (cin_hbm, wc.at[1]),
            (ce.at[0], ce.at[1]),
            (hd.at[0], hd.at[1]),
        ]
    ):
        swaps.append(
            pltpu.make_async_remote_copy(
                src_ref=src,
                dst_ref=dst,
                send_sem=wsend.at[i],
                recv_sem=wrecv.at[i],
                device_id=sib,
                device_id_type=MESH,
            )
        )
        swaps[-1].start()

    lane = iota((1, LANES), 1)
    base = 48 * (lane // 8) + lane % 8
    stacked = jnp.concatenate(
        [
            act_ref[...].reshape(1, 768).astype(F32),
            nact_ref[...].reshape(1, 768).astype(F32),
            jnp.zeros((6, 768), F32),
        ],
        axis=0,
    ).astype(BF16)
    columns = [
        jnp.broadcast_to(boot_ref[:, part * LANES : (part + 1) * LANES].astype(F32), (LANES, LANES)).T
        for part in range(6)
    ]
    for half in range(2):
        who = core if half == 0 else 1 - core
        for ch in range(CHUNKS):
            rows = base + 24 * who + 8 * ch
            pick = (iota((768, LANES), 0) == rows).astype(BF16)
            acts[half * CHUNKS + ch] = nn(stacked, pick)
            total = jnp.zeros((LANES, LANES), F32)
            for column in columns:
                total = total + (column == rows.astype(F32)).astype(F32)
            cnt[half * CHUNKS + ch] = jnp.broadcast_to(jnp.sum(total, axis=0, keepdims=True), (8, LANES))

    def hot_t(slot, row):
        return (iota((ACTS, LANES), 0).astype(F32) == acts[slot][row : row + 1]).astype(BF16)

    for ch in range(CHUNKS):
        ep[ch, 0] = tn(hot_t(ch, 0), em[0])
    swaps[0].wait_recv()
    swaps[1].wait_recv()
    for ch in range(CHUNKS):
        ep[ch, 1] = tn(hot_t(ch, 0), em[1])
    swaps[2].wait_recv()

    for ch in range(CHUNKS):
        if ch % AG1_GROUP == 0:
            landed(ag1, a_recv, ch, AG1_GROUP)
        x = jnp.concatenate([unfold(ag1[j, ch].astype(F32)) for j in range(CHIPS)], axis=0).astype(BF16)
        xs[0, ch] = x
        pltpu.make_async_remote_copy(
            src_ref=xs.at[0, ch],
            dst_ref=xs.at[1, ch],
            send_sem=x_send.at[ch],
            recv_sem=x_recv.at[ch],
            device_id=sib,
            device_id_type=MESH,
        ).start()
        inc = jnp.zeros((LANES, WIDTH), F32)
        for s in range(2):
            pre = nn(x, wi[s]) + ep[ch, s]
            inc = inc + nn((pre * sigmoid(pre)).astype(BF16), wo[s])
        for j in range(CHIPS):
            rss[j, ch] = fold(inc[j * 8 : j * 8 + 8]).astype(BF16)
        rsr[me, ch] = rss[me, ch]
        if (ch + 1) % RS_GROUP == 0:
            spread(lambda chip: rss.at[chip], rsr, r_send, r_recv, ch + 1 - RS_GROUP, RS_GROUP)

    for i in range(3, 6):
        swaps[i].wait_recv()
    for s in range(2):
        wct[s * LANES : (s + 1) * LANES] = wc[s].T
    wct[256:272] = jnp.concatenate([rhead_ref[...].astype(F32), jnp.zeros((15, WIDTH), F32)], axis=0).astype(BF16)
    heads = [jnp.broadcast_to(hd[s][:1], (LANES, LANES)).T for s in range(2)]
    for ch in range(CHUNKS):
        for s in range(2):
            ecn[ch, s] = tn(ce[s], hot_t(ch, 1))
            ecb[ch, s] = tn(ce[s], hot_t(ch, 0))
        ecb[CHUNKS + ch, 0] = tn(ce[0], hot_t(CHUNKS + ch, 0))

    def own_units(slot, pre):
        gate = sigmoid(pre)
        act = pre * gate
        at[slot] = act
        gt[slot] = heads[0] * (gate * (1.0 + pre * (1.0 - gate)))
        return act

    for ch in range(CHUNKS):
        x = xs[0, ch]
        pre = nt(wct[:256], x)
        act0 = own_units(ch, pre[:LANES] + ecb[ch, 0])
        pre1 = pre[LANES:] + ecb[ch, 1]
        weighted = act0 * heads[0] + pre1 * sigmoid(pre1) * heads[1]
        qv[ch : ch + 1] = jnp.sum(weighted, axis=0, keepdims=True)
        xt[:, ch * LANES : (ch + 1) * LANES] = x.T

    for swap in swaps:
        swap.wait_send()
    for first in range(0, CHUNKS, AG1_GROUP):
        landed(ag1, a_send, first, AG1_GROUP)

    for ch in range(CHUNKS):
        if ch % RS_GROUP == 0:
            landed(rsr, r_recv, ch, RS_GROUP)
        total = rsr[0, ch].astype(F32)
        for j in range(1, CHIPS):
            total = total + rsr[j, ch].astype(F32)
        ag2[me, ch] = (ag1[me, ch].astype(F32) + total).astype(BF16)
        if (ch + 1) % AG2_GROUP == 0:
            spread(lambda chip: ag2.at[me], ag2, n_send, n_recv, ch + 1 - AG2_GROUP, AG2_GROUP)

    for ch in range(CHUNKS):
        pltpu.make_async_copy(xs.at[1, ch], xs.at[1, ch], x_recv.at[ch]).wait()
        x = xs[1, ch]
        own_units(CHUNKS + ch, nt(wct[:LANES], x) + ecb[CHUNKS + ch, 0])
        xt[:, (CHUNKS + ch) * LANES : (CHUNKS + ch + 1) * LANES] = x.T

    for ch in range(CHUNKS):
        pltpu.make_async_copy(xs.at[0, ch], xs.at[0, ch], x_send.at[ch]).wait()
    for first in range(0, CHUNKS, RS_GROUP):
        landed(rss, r_send, first, RS_GROUP)

    for ch in range(CHUNKS):
        if ch % AG2_GROUP == 0:
            landed(ag2, n_recv, ch, AG2_GROUP)
        x = jnp.concatenate([unfold(ag2[j, ch].astype(F32)) for j in range(CHIPS)], axis=0).astype(BF16)
        pre = nt(wct[...], x)
        pre0 = pre[:LANES] + ecn[ch, 0]
        pre1 = pre[LANES:256] + ecn[ch, 1]
        weighted = pre0 * sigmoid(pre0) * heads[0] + pre1 * sigmoid(pre1) * heads[1]
        value = jnp.sum(weighted, axis=0, keepdims=True)
        ph6[me, ch : ch + 1] = discount * value + jnp.where(lane // 8 == me, pre[256:257], 0.0)
    ph6[me, 3:6] = qv[0:3]

    def share(other, step):
        return pltpu.make_async_remote_copy(
            src_ref=ph6.at[me],
            dst_ref=ph6.at[other * CHIPS + me],
            send_sem=s_send.at[0],
            recv_sem=s_recv.at[0],
            device_id=peer(step, other)[1],
            device_id_type=MESH,
        )

    for other, step in PLANE_ORDER:
        share(other, step).start()
    for first in range(0, CHUNKS, AG2_GROUP):
        landed(ag2, n_send, first, AG2_GROUP)
    slots = ph6.at[pl.ds(0, 31)]
    pltpu.make_async_copy(slots, slots, s_recv.at[0]).wait()
    halves = []
    for half in range(2):
        sums = ph6[half * CHIPS]
        for j in range(1, CHIPS):
            sums = sums + ph6[half * CHIPS + j]
        halves.append(sums)
    zb[zi] = jnp.concatenate([halves[0][:3], halves[1][:3], jnp.zeros((2, LANES), F32)], axis=0)
    for step in Z_ORDER:
        pltpu.make_async_remote_copy(
            src_ref=zb.at[zi],
            dst_ref=zb.at[zi],
            send_sem=s_send.at[1],
            recv_sem=s_recv.at[1],
            device_id=(dp, (zi + step) % MEMBERS),
            device_id_type=MESH,
        ).start()
    slots = ph6.at[pl.ds(0, 31)]
    pltpu.make_async_copy(slots, slots, s_send.at[0]).wait()
    slots = zb.at[pl.ds(0, MEMBERS - 1)]
    pltpu.make_async_copy(slots, slots, s_recv.at[1]).wait()
    total = zb[0]
    square = total * total
    for m in range(1, MEMBERS):
        one = zb[m]
        total = total + one
        square = square + one * one
    mean = total / MEMBERS
    spread = square / MEMBERS - mean * mean
    target = mean - penalty_weight * jnp.sqrt(spread + 1.0)

    turned = pltpu.roll(target, (LANES - 8 * me) % LANES, 1)
    line = turned[0:1]
    for ch in range(1, CHUNKS):
        line = jnp.where(lane // 8 == ch, pltpu.roll(turned, 8 * ch, 1)[ch : ch + 1], line)
    tgt_ref[...] = line[:, :24]

    head_sum = jnp.zeros((LANES, LANES), F32)
    for half in range(2):
        for ch in range(CHUNKS):
            slot = half * CHUNKS + ch
            scaled = cnt[slot][:1] * (halves[half][3 + ch : 4 + ch] - target[slot : slot + 1])
            head_sum = head_sum + scaled * at[slot]
            bt[:, slot * LANES : (slot + 1) * LANES] = (scaled * gt[slot]).astype(BF16)
    back = bt[...]
    gin_ref[...] = nt(xt[...], back)
    hots = jnp.concatenate([hot_t(slot, 0) for slot in range(2 * CHUNKS)], axis=1)
    gemb_ref[...] = nt(hots, back)[:18].reshape(18, 1, LANES)
    ghead_ref[...] = jnp.sum(head_sum.T, axis=0, keepdims=True)

    slots = zb.at[pl.ds(0, MEMBERS - 1)]
    pltpu.make_async_copy(slots, slots, s_send.at[1]).wait()


def finish(gin_ref, gemb_ref, ghead_ref, tgt_ref, gin_out, gemb_out, ghead_out, tgt_out, sem):
    copies = [
        pltpu.make_async_copy(src, dst, sem.at[i])
        for i, (src, dst) in enumerate(
            [(gin_ref, gin_out), (gemb_ref, gemb_out), (ghead_ref, ghead_out), (tgt_ref, tgt_out)]
        )
    ]
    for copy in copies:
        copy.start()
    for copy in copies:
        copy.wait()


def local(
    logged,
    row_ids,
    actions,
    next_actions,
    boot,
    dyn_in,
    dyn_embed,
    dyn_out,
    reward_head,
    critic_in,
    critic_embed,
    critic_head,
):
    vmem = pl.BlockSpec(memory_space=pltpu.VMEM)
    hbm = pl.BlockSpec(memory_space=pltpu.HBM)
    dma = pltpu.SemaphoreType.DMA
    blocks = (CHIPS, CHUNKS, 16, HALF)
    shapes = (
        jax.ShapeDtypeStruct((WIDTH, LANES), F32),
        jax.ShapeDtypeStruct((18, 1, LANES), F32),
        jax.ShapeDtypeStruct((1, LANES), F32),
        jax.ShapeDtypeStruct((1, 24), F32),
    )
    results = pl.pallas_call(
        kernel,
        out_shape=shapes,
        in_specs=[hbm] * 12,
        out_specs=(vmem,) * 4,
        scratch_shapes=[
            pltpu.VMEM((24,), jnp.int32),
            pltpu.VMEM((768,), jnp.int32),
            pltpu.VMEM((768,), jnp.int32),
            pltpu.VMEM((1, 768), jnp.int32),
            pltpu.VMEM((1, WIDTH), BF16),
            pltpu.VMEM((1, LANES), BF16),
            pltpu.VMEM((18, 256), BF16),
            pltpu.VMEM((18, LANES), BF16),
            pltpu.VMEM((256, WIDTH), BF16),
            pltpu.VMEM((2, WIDTH, 256), BF16),
            pltpu.VMEM((2, 256, WIDTH), BF16),
            pltpu.VMEM((2, WIDTH, LANES), BF16),
            pltpu.VMEM((2, ACTS, 256), BF16),
            pltpu.VMEM((2, ACTS, LANES), BF16),
            pltpu.VMEM((2, 8, LANES), F32),
            pltpu.VMEM(blocks, BF16),
            pltpu.VMEM((2, CHUNKS, LANES, WIDTH), BF16),
            pltpu.VMEM((CHUNKS, 2, LANES, 256), F32),
            pltpu.VMEM(blocks, BF16),
            pltpu.VMEM(blocks, BF16),
            pltpu.VMEM(blocks, BF16),
            pltpu.VMEM((272, WIDTH), BF16),
            pltpu.VMEM((CHUNKS, 2, LANES, LANES), F32),
            pltpu.VMEM((2 * CHUNKS, 2, LANES, LANES), F32),
            pltpu.VMEM((2 * CHUNKS, LANES, LANES), F32),
            pltpu.VMEM((2 * CHUNKS, LANES, LANES), F32),
            pltpu.VMEM((WIDTH, 768), BF16),
            pltpu.VMEM((LANES, 768), BF16),
            pltpu.VMEM((2 * CHUNKS, 8, LANES), F32),
            pltpu.VMEM((2 * CHUNKS, 8, LANES), F32),
            pltpu.VMEM((8, LANES), F32),
            pltpu.VMEM((2 * CHIPS, 8, LANES), F32),
            pltpu.VMEM((MEMBERS, 8, LANES), F32),
            dma((12,)),
            dma((6,)),
            dma((6,)),
            dma((CHUNKS,)),
            dma((CHUNKS,)),
            dma((CHUNKS,)),
            dma((CHUNKS,)),
            dma((CHUNKS,)),
            dma((CHUNKS,)),
            dma((CHUNKS,)),
            dma((CHUNKS,)),
            dma((2,)),
            dma((2,)),
        ],
        compiler_params=pltpu.CompilerParams(
            collective_id=0, has_side_effects=True, vmem_limit_bytes=60 * 2**20
        ),
        name="rollout",
    )(
        row_ids,
        actions,
        next_actions,
        boot,
        reward_head,
        critic_head,
        dyn_embed[0],
        critic_embed[0],
        logged,
        dyn_in[0],
        dyn_out[0],
        critic_in[0],
    )
    grad_in, grad_embed, grad_head, target = pl.pallas_call(
        finish,
        out_shape=shapes,
        in_specs=[vmem] * 4,
        out_specs=(hbm,) * 4,
        scratch_shapes=[dma((4,))],
        compiler_params=pltpu.CompilerParams(vmem_limit_bytes=60 * 2**20),
        name="finish",
    )(*results)
    return grad_in[None], grad_embed.transpose(1, 0, 2), grad_head, target[0]


def solution(mesh):
    return jax.shard_map(
        local,
        mesh=mesh,
        in_specs=(
            P("dp", None),
            P("dp"),
            P(),
            P(),
            P("mp", None),
            P("mp", None, "dp"),
            P("mp", None, "dp"),
            P("mp", "dp", None),
            P("mp", None),
            P("mp", None, "dp"),
            P("mp", None, "dp"),
            P("mp", "dp"),
        ),
        out_specs=(P("mp", None, "dp"), P("mp", None, "dp"), P("mp", "dp"), P("dp")),
        check_vma=False,
    )
```

```python
import jax
import jax.numpy as jnp
from jax import lax
from jax.experimental import pallas as pl
from jax.experimental.pallas import tpu as pltpu
from jax.sharding import PartitionSpec as P

MESH = pl.DeviceIdType.MESH
F32 = jnp.float32
BF16 = jnp.bfloat16

discount = 0.99
penalty_weight = 1.0

CHUNKS = 3
CHIPS = 16
SIDE = 4
MEMBERS = 16
WIDTH = 1024
HALF = 512
LANES = 128
ACTS = 32

AG1_GROUP = 1
RS_GROUP = 1
AG2_GROUP = 1

HOPS = (0, 1, 2, 1)
PLANE_ORDER = sorted(
    [(other, step) for other in range(2) for step in range(CHIPS) if other or step],
    key=lambda pair: (-HOPS[pair[1] // SIDE] - HOPS[pair[1] % SIDE], pair),
)
Z_ORDER = (8, 7, 9, 6, 10, 5, 11, 4, 12, 3, 13, 2, 14, 1, 15)


def nt(lhs, rhs):
    return lax.dot_general(lhs, rhs, (((1,), (1,)), ((), ())), preferred_element_type=F32)


def tn(lhs, rhs):
    return lax.dot_general(lhs, rhs, (((0,), (0,)), ((), ())), preferred_element_type=F32)


def nn(lhs, rhs):
    return jnp.dot(lhs, rhs, preferred_element_type=F32)


def sigmoid(v):
    return 0.5 * jnp.tanh(0.5 * v) + 0.5


def fold(block):
    return jnp.concatenate([block[:, :HALF], block[:, HALF:]], axis=0)


def unfold(block):
    return jnp.concatenate([block[:8], block[8:]], axis=1)


def iota(shape, dim):
    return lax.broadcasted_iota(jnp.int32, shape, dim)


def kernel(
    rowid_hbm,
    act_hbm,
    nact_hbm,
    boot_hbm,
    rhead_hbm,
    chead_hbm,
    demb_hbm,
    cemb_hbm,
    logged_hbm,
    din_hbm,
    dout_hbm,
    cin_hbm,
    gin_ref,
    gemb_ref,
    ghead_ref,
    tgt_ref,
    rowid_ref,
    act_ref,
    nact_ref,
    boot_ref,
    rhead_ref,
    chead_ref,
    demb_ref,
    cemb_ref,
    logv,
    wi,
    wo,
    wc,
    em,
    ce,
    hd,
    ag1,
    xs,
    ep,
    rss,
    rsr,
    ag2,
    wct,
    ecn,
    ecb,
    at,
    gt,
    xt,
    bt,
    acts,
    cnt,
    qv,
    ph6,
    zb,
    loc_sem,
    wsend,
    wrecv,
    a_send,
    a_recv,
    r_send,
    r_recv,
    n_send,
    n_recv,
    x_send,
    x_recv,
    s_send,
    s_recv,
):
    dp = lax.axis_index("dp")
    zi = lax.axis_index("mp")
    core = dp % 2
    me = dp // 2
    px = me % SIDE
    py = me // SIDE
    sib = (dp + 1 - 2 * core, zi)

    def peer(step, other=0):
        chip = ((py + step // SIDE) % SIDE) * SIDE + (px + step % SIDE) % SIDE
        return chip, (chip * 2 + (core + other) % 2, zi)

    loads = [
        pltpu.make_async_copy(src, dst, loc_sem.at[i])
        for i, (src, dst) in enumerate(
            [
                (logged_hbm, logv),
                (rowid_hbm, rowid_ref),
                (demb_hbm, demb_ref),
                (cemb_hbm, cemb_ref),
                (chead_hbm, chead_ref),
                (act_hbm, act_ref),
                (nact_hbm, nact_ref),
                (boot_hbm, boot_ref),
                (rhead_hbm, rhead_ref),
                (din_hbm, wi.at[0]),
                (dout_hbm, wo.at[0]),
                (cin_hbm, wc.at[0]),
            ]
        )
    ]
    for load in loads[:2]:
        load.start()

    barrier = pltpu.get_barrier_semaphore()
    for step in Z_ORDER:
        pl.semaphore_signal(barrier, inc=1, device_id=(dp, (zi + step) % MEMBERS), device_id_type=MESH)
    for other, step in PLANE_ORDER:
        pl.semaphore_signal(barrier, inc=1, device_id=peer(step, other)[1], device_id_type=MESH)
    for load in loads[2:]:
        load.start()

    loads[0].wait()
    loads[1].wait()
    hot = (iota((256, 24), 0) == rowid_ref[...]).astype(BF16)
    picked = tn(hot, logv[...])
    for ch in range(CHUNKS):
        ag1[me, ch] = fold(picked[ch * 8 : ch * 8 + 8]).astype(BF16)
    pl.semaphore_wait(barrier, 31 + MEMBERS - 1)

    def spread(src, dst, send_sem, recv_sem, first, count):
        def one(step):
            chip, where = peer(step)
            pltpu.make_async_remote_copy(
                src_ref=src(chip).at[pl.ds(first, count)],
                dst_ref=dst.at[me, pl.ds(first, count)],
                send_sem=send_sem.at[first],
                recv_sem=recv_sem.at[first],
                device_id=where,
                device_id_type=MESH,
            ).start()

        for other, step in PLANE_ORDER:
            if other == 0:
                one(step)

    def landed(buf, sem, first, count):
        slots = buf.at[pl.ds(0, CHIPS - 1), pl.ds(first, count)]
        pltpu.make_async_copy(slots, slots, sem.at[first]).wait()

    for first in range(0, CHUNKS, AG1_GROUP):
        spread(lambda chip: ag1.at[me], ag1, a_send, a_recv, first, AG1_GROUP)

    for load in loads[2:]:
        load.wait()
    eye = (iota((ACTS, 18), 0) == iota((ACTS, 18), 1)).astype(BF16)
    em[0] = nn(eye, demb_ref[...]).astype(BF16)
    ce[0] = nn(eye, cemb_ref[...]).astype(BF16)
    hd[0] = jnp.broadcast_to(chead_ref[...].astype(F32), (8, LANES))

    swaps = []
    for i, (src, dst) in enumerate(
        [
            (din_hbm, wi.at[1]),
            (em.at[0], em.at[1]),
            (dout_hbm, wo.at[1]),
            (cin_hbm, wc.at[1]),
            (ce.at[0], ce.at[1]),
            (hd.at[0], hd.at[1]),
        ]
    ):
        swaps.append(
            pltpu.make_async_remote_copy(
                src_ref=src,
                dst_ref=dst,
                send_sem=wsend.at[i],
                recv_sem=wrecv.at[i],
                device_id=sib,
                device_id_type=MESH,
            )
        )
        swaps[-1].start()

    lane = iota((1, LANES), 1)
    base = 48 * (lane // 8) + lane % 8
    stacked = jnp.concatenate(
        [
            act_ref[...].reshape(1, 768).astype(F32),
            nact_ref[...].reshape(1, 768).astype(F32),
            jnp.zeros((6, 768), F32),
        ],
        axis=0,
    ).astype(BF16)
    columns = [
        jnp.broadcast_to(boot_ref[:, part * LANES : (part + 1) * LANES].astype(F32), (LANES, LANES)).T
        for part in range(6)
    ]
    for half in range(2):
        who = core if half == 0 else 1 - core
        for ch in range(CHUNKS):
            rows = base + 24 * who + 8 * ch
            pick = (iota((768, LANES), 0) == rows).astype(BF16)
            acts[half * CHUNKS + ch] = nn(stacked, pick)
            total = jnp.zeros((LANES, LANES), F32)
            for column in columns:
                total = total + (column == rows.astype(F32)).astype(F32)
            cnt[half * CHUNKS + ch] = jnp.broadcast_to(jnp.sum(total, axis=0, keepdims=True), (8, LANES))

    def hot_t(slot, row):
        return (iota((ACTS, LANES), 0).astype(F32) == acts[slot][row : row + 1]).astype(BF16)

    for ch in range(CHUNKS):
        ep[ch, 0] = tn(hot_t(ch, 0), em[0])
    swaps[0].wait_recv()
    swaps[1].wait_recv()
    for ch in range(CHUNKS):
        ep[ch, 1] = tn(hot_t(ch, 0), em[1])
    swaps[2].wait_recv()

    for ch in range(CHUNKS):
        if ch % AG1_GROUP == 0:
            landed(ag1, a_recv, ch, AG1_GROUP)
        x = jnp.concatenate([unfold(ag1[j, ch].astype(F32)) for j in range(CHIPS)], axis=0).astype(BF16)
        xs[0, ch] = x
        pltpu.make_async_remote_copy(
            src_ref=xs.at[0, ch],
            dst_ref=xs.at[1, ch],
            send_sem=x_send.at[ch],
            recv_sem=x_recv.at[ch],
            device_id=sib,
            device_id_type=MESH,
        ).start()
        inc = jnp.zeros((LANES, WIDTH), F32)
        for s in range(2):
            pre = nn(x, wi[s]) + ep[ch, s]
            inc = inc + nn((pre * sigmoid(pre)).astype(BF16), wo[s])
        for j in range(CHIPS):
            rss[j, ch] = fold(inc[j * 8 : j * 8 + 8]).astype(BF16)
        rsr[me, ch] = rss[me, ch]
        if (ch + 1) % RS_GROUP == 0:
            spread(lambda chip: rss.at[chip], rsr, r_send, r_recv, ch + 1 - RS_GROUP, RS_GROUP)

    for i in range(3, 6):
        swaps[i].wait_recv()
    for s in range(2):
        wct[s * LANES : (s + 1) * LANES] = wc[s].T
    wct[256:272] = jnp.concatenate([rhead_ref[...].astype(F32), jnp.zeros((15, WIDTH), F32)], axis=0).astype(BF16)
    heads = [jnp.broadcast_to(hd[s][:1], (LANES, LANES)).T for s in range(2)]
    for ch in range(CHUNKS):
        for s in range(2):
            ecn[ch, s] = tn(ce[s], hot_t(ch, 1))
            ecb[ch, s] = tn(ce[s], hot_t(ch, 0))
        ecb[CHUNKS + ch, 0] = tn(ce[0], hot_t(CHUNKS + ch, 0))

    def own_units(slot, pre):
        gate = sigmoid(pre)
        act = pre * gate
        at[slot] = act
        gt[slot] = heads[0] * (gate * (1.0 + pre * (1.0 - gate)))
        return act

    for ch in range(CHUNKS):
        x = xs[0, ch]
        pre = nt(wct[:256], x)
        act0 = own_units(ch, pre[:LANES] + ecb[ch, 0])
        pre1 = pre[LANES:] + ecb[ch, 1]
        weighted = act0 * heads[0] + pre1 * sigmoid(pre1) * heads[1]
        qv[ch : ch + 1] = jnp.sum(weighted, axis=0, keepdims=True)
        xt[:, ch * LANES : (ch + 1) * LANES] = x.T

    for swap in swaps:
        swap.wait_send()
    for first in range(0, CHUNKS, AG1_GROUP):
        landed(ag1, a_send, first, AG1_GROUP)

    for ch in range(CHUNKS):
        if ch % RS_GROUP == 0:
            landed(rsr, r_recv, ch, RS_GROUP)
        total = rsr[0, ch].astype(F32)
        for j in range(1, CHIPS):
            total = total + rsr[j, ch].astype(F32)
        ag2[me, ch] = (ag1[me, ch].astype(F32) + total).astype(BF16)
        if (ch + 1) % AG2_GROUP == 0:
            spread(lambda chip: ag2.at[me], ag2, n_send, n_recv, ch + 1 - AG2_GROUP, AG2_GROUP)

    for ch in range(CHUNKS):
        pltpu.make_async_copy(xs.at[1, ch], xs.at[1, ch], x_recv.at[ch]).wait()
        x = xs[1, ch]
        own_units(CHUNKS + ch, nt(wct[:LANES], x) + ecb[CHUNKS + ch, 0])
        xt[:, (CHUNKS + ch) * LANES : (CHUNKS + ch + 1) * LANES] = x.T

    for ch in range(CHUNKS):
        pltpu.make_async_copy(xs.at[0, ch], xs.at[0, ch], x_send.at[ch]).wait()
    for first in range(0, CHUNKS, RS_GROUP):
        landed(rss, r_send, first, RS_GROUP)

    for ch in range(CHUNKS):
        if ch % AG2_GROUP == 0:
            landed(ag2, n_recv, ch, AG2_GROUP)
        x = jnp.concatenate([unfold(ag2[j, ch].astype(F32)) for j in range(CHIPS)], axis=0).astype(BF16)
        pre = nt(wct[...], x)
        pre0 = pre[:LANES] + ecn[ch, 0]
        pre1 = pre[LANES:256] + ecn[ch, 1]
        weighted = pre0 * sigmoid(pre0) * heads[0] + pre1 * sigmoid(pre1) * heads[1]
        value = jnp.sum(weighted, axis=0, keepdims=True)
        ph6[me, ch : ch + 1] = discount * value + jnp.where(lane // 8 == me, pre[256:257], 0.0)
    ph6[me, 3:6] = qv[0:3]

    def share(other, step):
        return pltpu.make_async_remote_copy(
            src_ref=ph6.at[me],
            dst_ref=ph6.at[other * CHIPS + me],
            send_sem=s_send.at[0],
            recv_sem=s_recv.at[0],
            device_id=peer(step, other)[1],
            device_id_type=MESH,
        )

    for other, step in PLANE_ORDER:
        share(other, step).start()
    for first in range(0, CHUNKS, AG2_GROUP):
        landed(ag2, n_send, first, AG2_GROUP)
    slots = ph6.at[pl.ds(0, 31)]
    pltpu.make_async_copy(slots, slots, s_recv.at[0]).wait()
    halves = []
    for half in range(2):
        sums = ph6[half * CHIPS]
        for j in range(1, CHIPS):
            sums = sums + ph6[half * CHIPS + j]
        halves.append(sums)
    zb[zi] = jnp.concatenate([halves[0][:3], halves[1][:3], jnp.zeros((2, LANES), F32)], axis=0)
    for step in Z_ORDER:
        pltpu.make_async_remote_copy(
            src_ref=zb.at[zi],
            dst_ref=zb.at[zi],
            send_sem=s_send.at[1],
            recv_sem=s_recv.at[1],
            device_id=(dp, (zi + step) % MEMBERS),
            device_id_type=MESH,
        ).start()
    slots = ph6.at[pl.ds(0, 31)]
    pltpu.make_async_copy(slots, slots, s_send.at[0]).wait()
    slots = zb.at[pl.ds(0, MEMBERS - 1)]
    pltpu.make_async_copy(slots, slots, s_recv.at[1]).wait()
    total = zb[0]
    square = total * total
    for m in range(1, MEMBERS):
        one = zb[m]
        total = total + one
        square = square + one * one
    mean = total / MEMBERS
    spread = square / MEMBERS - mean * mean
    target = mean - penalty_weight * jnp.sqrt(spread + 1.0)

    turned = pltpu.roll(target, (LANES - 8 * me) % LANES, 1)
    line = turned[0:1]
    for ch in range(1, CHUNKS):
        line = jnp.where(lane // 8 == ch, pltpu.roll(turned, 8 * ch, 1)[ch : ch + 1], line)
    tgt_ref[...] = line[:, :24]

    head_sum = jnp.zeros((LANES, LANES), F32)
    for half in range(2):
        for ch in range(CHUNKS):
            slot = half * CHUNKS + ch
            scaled = cnt[slot][:1] * (halves[half][3 + ch : 4 + ch] - target[slot : slot + 1])
            head_sum = head_sum + scaled * at[slot]
            bt[:, slot * LANES : (slot + 1) * LANES] = (scaled * gt[slot]).astype(BF16)
    back = bt[...]
    gin_ref[...] = nt(xt[...], back)
    hots = jnp.concatenate([hot_t(slot, 0) for slot in range(2 * CHUNKS)], axis=1)
    gemb_ref[...] = nt(hots, back).reshape(ACTS, 1, LANES)
    ghead_ref[...] = jnp.sum(head_sum.T, axis=0, keepdims=True)

    slots = zb.at[pl.ds(0, MEMBERS - 1)]
    pltpu.make_async_copy(slots, slots, s_send.at[1]).wait()


def finish(gin_ref, gemb_ref, ghead_ref, tgt_ref, gin_out, gemb_out, ghead_out, tgt_out, sem):
    copies = [
        pltpu.make_async_copy(src, dst, sem.at[i])
        for i, (src, dst) in enumerate(
            [(gin_ref, gin_out), (gemb_ref.at[pl.ds(0, 18)], gemb_out), (ghead_ref, ghead_out), (tgt_ref, tgt_out)]
        )
    ]
    for copy in copies:
        copy.start()
    for copy in copies:
        copy.wait()


def local(
    logged,
    row_ids,
    actions,
    next_actions,
    boot,
    dyn_in,
    dyn_embed,
    dyn_out,
    reward_head,
    critic_in,
    critic_embed,
    critic_head,
):
    vmem = pl.BlockSpec(memory_space=pltpu.VMEM)
    hbm = pl.BlockSpec(memory_space=pltpu.HBM)
    dma = pltpu.SemaphoreType.DMA
    blocks = (CHIPS, CHUNKS, 16, HALF)
    def shapes(rows):
        return tuple(
            jax.ShapeDtypeStruct(shape, F32) for shape in ((WIDTH, LANES), (rows, 1, LANES), (1, LANES), (1, 24))
        )

    results = pl.pallas_call(
        kernel,
        out_shape=shapes(ACTS),
        in_specs=[hbm] * 12,
        out_specs=(vmem,) * 4,
        scratch_shapes=[
            pltpu.VMEM((1, 24), jnp.int32),
            pltpu.VMEM((768,), jnp.int32),
            pltpu.VMEM((768,), jnp.int32),
            pltpu.VMEM((1, 768), jnp.int32),
            pltpu.VMEM((1, WIDTH), BF16),
            pltpu.VMEM((1, LANES), BF16),
            pltpu.VMEM((18, 256), BF16),
            pltpu.VMEM((18, LANES), BF16),
            pltpu.VMEM((256, WIDTH), BF16),
            pltpu.VMEM((2, WIDTH, 256), BF16),
            pltpu.VMEM((2, 256, WIDTH), BF16),
            pltpu.VMEM((2, WIDTH, LANES), BF16),
            pltpu.VMEM((2, ACTS, 256), BF16),
            pltpu.VMEM((2, ACTS, LANES), BF16),
            pltpu.VMEM((2, 8, LANES), F32),
            pltpu.VMEM(blocks, BF16),
            pltpu.VMEM((2, CHUNKS, LANES, WIDTH), BF16),
            pltpu.VMEM((CHUNKS, 2, LANES, 256), F32),
            pltpu.VMEM(blocks, BF16),
            pltpu.VMEM(blocks, BF16),
            pltpu.VMEM(blocks, BF16),
            pltpu.VMEM((272, WIDTH), BF16),
            pltpu.VMEM((CHUNKS, 2, LANES, LANES), F32),
            pltpu.VMEM((2 * CHUNKS, 2, LANES, LANES), F32),
            pltpu.VMEM((2 * CHUNKS, LANES, LANES), F32),
            pltpu.VMEM((2 * CHUNKS, LANES, LANES), F32),
            pltpu.VMEM((WIDTH, 768), BF16),
            pltpu.VMEM((LANES, 768), BF16),
            pltpu.VMEM((2 * CHUNKS, 8, LANES), F32),
            pltpu.VMEM((2 * CHUNKS, 8, LANES), F32),
            pltpu.VMEM((8, LANES), F32),
            pltpu.VMEM((2 * CHIPS, 8, LANES), F32),
            pltpu.VMEM((MEMBERS, 8, LANES), F32),
            dma((12,)),
            dma((6,)),
            dma((6,)),
            dma((CHUNKS,)),
            dma((CHUNKS,)),
            dma((CHUNKS,)),
            dma((CHUNKS,)),
            dma((CHUNKS,)),
            dma((CHUNKS,)),
            dma((CHUNKS,)),
            dma((CHUNKS,)),
            dma((2,)),
            dma((2,)),
        ],
        compiler_params=pltpu.CompilerParams(
            collective_id=0, has_side_effects=True, vmem_limit_bytes=60 * 2**20
        ),
        name="rollout",
    )(
        row_ids[None],
        actions,
        next_actions,
        boot,
        reward_head,
        critic_head,
        dyn_embed[0],
        critic_embed[0],
        logged,
        dyn_in[0],
        dyn_out[0],
        critic_in[0],
    )
    grad_in, grad_embed, grad_head, target = pl.pallas_call(
        finish,
        out_shape=shapes(18),
        in_specs=[vmem] * 4,
        out_specs=(hbm,) * 4,
        scratch_shapes=[dma((4,))],
        compiler_params=pltpu.CompilerParams(vmem_limit_bytes=60 * 2**20),
        name="finish",
    )(*results)
    return grad_in[None], grad_embed.transpose(1, 0, 2), grad_head, target[0]


def solution(mesh):
    return jax.shard_map(
        local,
        mesh=mesh,
        in_specs=(
            P("dp", None),
            P("dp"),
            P(),
            P(),
            P("mp", None),
            P("mp", None, "dp"),
            P("mp", None, "dp"),
            P("mp", "dp", None),
            P("mp", None),
            P("mp", None, "dp"),
            P("mp", None, "dp"),
            P("mp", "dp"),
        ),
        out_specs=(P("mp", None, "dp"), P("mp", None, "dp"), P("mp", "dp"), P("dp")),
        check_vma=False,
    )
```

```python
import jax
import jax.numpy as jnp
from jax import lax
from jax.experimental import pallas as pl
from jax.experimental.pallas import tpu as pltpu
from jax.sharding import PartitionSpec as P

MESH = pl.DeviceIdType.MESH
F32 = jnp.float32
BF16 = jnp.bfloat16

discount = 0.99
penalty_weight = 1.0

CHUNKS = 3
CHIPS = 16
SIDE = 4
MEMBERS = 16
WIDTH = 1024
HALF = 512
LANES = 128
ACTS = 32

AG1_GROUP = 1
RS_GROUP = 1
AG2_GROUP = 1

HOPS = (0, 1, 2, 1)
PLANE_ORDER = sorted(
    [(other, step) for other in range(2) for step in range(CHIPS) if other or step],
    key=lambda pair: (-HOPS[pair[1] // SIDE] - HOPS[pair[1] % SIDE], pair),
)
Z_ORDER = (8, 7, 9, 6, 10, 5, 11, 4, 12, 3, 13, 2, 14, 1, 15)


def nt(lhs, rhs):
    return lax.dot_general(lhs, rhs, (((1,), (1,)), ((), ())), preferred_element_type=F32)


def tn(lhs, rhs):
    return lax.dot_general(lhs, rhs, (((0,), (0,)), ((), ())), preferred_element_type=F32)


def nn(lhs, rhs):
    return jnp.dot(lhs, rhs, preferred_element_type=F32)


def sigmoid(v):
    return 0.5 * jnp.tanh(0.5 * v) + 0.5


def fold(block):
    return jnp.concatenate([block[:, :HALF], block[:, HALF:]], axis=0)


def unfold(block):
    return jnp.concatenate([block[:8], block[8:]], axis=1)


def iota(shape, dim):
    return lax.broadcasted_iota(jnp.int32, shape, dim)


def kernel(
    rowid_hbm,
    act_hbm,
    nact_hbm,
    boot_hbm,
    rhead_hbm,
    chead_hbm,
    demb_hbm,
    cemb_hbm,
    logged_hbm,
    din_hbm,
    dout_hbm,
    cin_hbm,
    gin_ref,
    gemb_ref,
    ghead_ref,
    tgt_ref,
    rowid_ref,
    act_ref,
    nact_ref,
    boot_ref,
    rhead_ref,
    chead_ref,
    demb_ref,
    cemb_ref,
    logv,
    wi,
    wo,
    wc,
    em,
    ce,
    hd,
    ag1,
    xs,
    ep,
    rss,
    rsr,
    ag2,
    wct,
    ecn,
    ecb,
    at,
    gt,
    xt,
    bt,
    acts,
    cnt,
    qv,
    ph6,
    zb,
    loc_sem,
    wsend,
    wrecv,
    a_send,
    a_recv,
    r_send,
    r_recv,
    n_send,
    n_recv,
    x_send,
    x_recv,
    s_send,
    s_recv,
):
    dp = lax.axis_index("dp")
    zi = lax.axis_index("mp")
    core = dp % 2
    me = dp // 2
    px = me % SIDE
    py = me // SIDE
    sib = (dp + 1 - 2 * core, zi)

    down = [(py + k) % SIDE * SIDE for k in range(SIDE)]
    across = [(px + k) % SIDE for k in range(SIDE)]
    cores = (core, 1 - core)
    along = [(zi + k) % MEMBERS for k in range(MEMBERS)]

    def peer(step, other=0):
        chip = down[step // SIDE] + across[step % SIDE]
        return chip, (2 * chip + cores[other], zi)

    loads = [
        pltpu.make_async_copy(src, dst, loc_sem.at[i])
        for i, (src, dst) in enumerate(
            [
                (logged_hbm, logv),
                (rowid_hbm, rowid_ref),
                (demb_hbm, demb_ref),
                (cemb_hbm, cemb_ref),
                (chead_hbm, chead_ref),
                (act_hbm, act_ref),
                (nact_hbm, nact_ref),
                (boot_hbm, boot_ref),
                (rhead_hbm, rhead_ref),
                (din_hbm, wi.at[0]),
                (dout_hbm, wo.at[0]),
                (cin_hbm, wc.at[0]),
            ]
        )
    ]
    for load in loads[:2]:
        load.start()

    barrier = pltpu.get_barrier_semaphore()
    for step in Z_ORDER:
        pl.semaphore_signal(barrier, inc=1, device_id=(dp, along[step]), device_id_type=MESH)
    for other, step in PLANE_ORDER:
        pl.semaphore_signal(barrier, inc=1, device_id=peer(step, other)[1], device_id_type=MESH)
    for load in loads[2:]:
        load.start()

    loads[0].wait()
    loads[1].wait()
    hot = (iota((256, 24), 0) == rowid_ref[...]).astype(BF16)
    picked = tn(hot, logv[...])
    for ch in range(CHUNKS):
        ag1[me, ch] = fold(picked[ch * 8 : ch * 8 + 8]).astype(BF16)
    pl.semaphore_wait(barrier, 31 + MEMBERS - 1)

    def spread(src, dst, send_sem, recv_sem, first, count):
        def one(step):
            chip, where = peer(step)
            pltpu.make_async_remote_copy(
                src_ref=src(chip).at[pl.ds(first, count)],
                dst_ref=dst.at[me, pl.ds(first, count)],
                send_sem=send_sem.at[first],
                recv_sem=recv_sem.at[first],
                device_id=where,
                device_id_type=MESH,
            ).start()

        for other, step in PLANE_ORDER:
            if other == 0:
                one(step)

    def landed(buf, sem, first, count):
        slots = buf.at[pl.ds(0, CHIPS - 1), pl.ds(first, count)]
        pltpu.make_async_copy(slots, slots, sem.at[first]).wait()

    for first in range(0, CHUNKS, AG1_GROUP):
        spread(lambda chip: ag1.at[me], ag1, a_send, a_recv, first, AG1_GROUP)

    for load in loads[2:]:
        load.wait()
    eye = (iota((ACTS, 18), 0) == iota((ACTS, 18), 1)).astype(BF16)
    em[0] = nn(eye, demb_ref[...]).astype(BF16)
    ce[0] = nn(eye, cemb_ref[...]).astype(BF16)
    hd[0] = jnp.broadcast_to(chead_ref[...].astype(F32), (8, LANES))

    swaps = []
    for i, (src, dst) in enumerate(
        [
            (din_hbm, wi.at[1]),
            (em.at[0], em.at[1]),
            (dout_hbm, wo.at[1]),
            (cin_hbm, wc.at[1]),
            (ce.at[0], ce.at[1]),
            (hd.at[0], hd.at[1]),
        ]
    ):
        swaps.append(
            pltpu.make_async_remote_copy(
                src_ref=src,
                dst_ref=dst,
                send_sem=wsend.at[i],
                recv_sem=wrecv.at[i],
                device_id=sib,
                device_id_type=MESH,
            )
        )
        swaps[-1].start()

    lane = iota((1, LANES), 1)
    base = 48 * (lane // 8) + lane % 8
    stacked = jnp.concatenate(
        [
            act_ref[...].reshape(1, 768).astype(F32),
            nact_ref[...].reshape(1, 768).astype(F32),
            jnp.zeros((6, 768), F32),
        ],
        axis=0,
    ).astype(BF16)
    columns = [
        jnp.broadcast_to(boot_ref[:, part * LANES : (part + 1) * LANES].astype(F32), (LANES, LANES)).T
        for part in range(6)
    ]
    for half in range(2):
        who = core if half == 0 else 1 - core
        for ch in range(CHUNKS):
            rows = base + 24 * who + 8 * ch
            pick = (iota((768, LANES), 0) == rows).astype(BF16)
            acts[half * CHUNKS + ch] = nn(stacked, pick)
            total = jnp.zeros((LANES, LANES), F32)
            for column in columns:
                total = total + (column == rows.astype(F32)).astype(F32)
            cnt[half * CHUNKS + ch] = jnp.broadcast_to(jnp.sum(total, axis=0, keepdims=True), (8, LANES))

    def hot_t(slot, row):
        return (iota((ACTS, LANES), 0).astype(F32) == acts[slot][row : row + 1]).astype(BF16)

    for ch in range(CHUNKS):
        ep[ch, 0] = tn(hot_t(ch, 0), em[0])
    swaps[0].wait_recv()
    swaps[1].wait_recv()
    for ch in range(CHUNKS):
        ep[ch, 1] = tn(hot_t(ch, 0), em[1])
    swaps[2].wait_recv()

    for ch in range(CHUNKS):
        if ch % AG1_GROUP == 0:
            landed(ag1, a_recv, ch, AG1_GROUP)
        x = jnp.concatenate([unfold(ag1[j, ch].astype(F32)) for j in range(CHIPS)], axis=0).astype(BF16)
        xs[0, ch] = x
        pltpu.make_async_remote_copy(
            src_ref=xs.at[0, ch],
            dst_ref=xs.at[1, ch],
            send_sem=x_send.at[ch],
            recv_sem=x_recv.at[ch],
            device_id=sib,
            device_id_type=MESH,
        ).start()
        inc = jnp.zeros((LANES, WIDTH), F32)
        for s in range(2):
            pre = nn(x, wi[s]) + ep[ch, s]
            inc = inc + nn((pre * sigmoid(pre)).astype(BF16), wo[s])
        for j in range(CHIPS):
            rss[j, ch] = fold(inc[j * 8 : j * 8 + 8]).astype(BF16)
        rsr[me, ch] = rss[me, ch]
        if (ch + 1) % RS_GROUP == 0:
            spread(lambda chip: rss.at[chip], rsr, r_send, r_recv, ch + 1 - RS_GROUP, RS_GROUP)

    for i in range(3, 6):
        swaps[i].wait_recv()
    for s in range(2):
        wct[s * LANES : (s + 1) * LANES] = wc[s].T
    wct[256:272] = jnp.concatenate([rhead_ref[...].astype(F32), jnp.zeros((15, WIDTH), F32)], axis=0).astype(BF16)
    heads = [jnp.broadcast_to(hd[s][:1], (LANES, LANES)).T for s in range(2)]
    for ch in range(CHUNKS):
        for s in range(2):
            ecn[ch, s] = tn(ce[s], hot_t(ch, 1))
            ecb[ch, s] = tn(ce[s], hot_t(ch, 0))
        ecb[CHUNKS + ch, 0] = tn(ce[0], hot_t(CHUNKS + ch, 0))

    def own_units(slot, pre):
        gate = sigmoid(pre)
        act = pre * gate
        at[slot] = act
        gt[slot] = heads[0] * (gate * (1.0 + pre * (1.0 - gate)))
        return act

    for ch in range(CHUNKS):
        x = xs[0, ch]
        pre = nt(wct[:256], x)
        act0 = own_units(ch, pre[:LANES] + ecb[ch, 0])
        pre1 = pre[LANES:] + ecb[ch, 1]
        weighted = act0 * heads[0] + pre1 * sigmoid(pre1) * heads[1]
        qv[ch : ch + 1] = jnp.sum(weighted, axis=0, keepdims=True)
        xt[:, ch * LANES : (ch + 1) * LANES] = x.T

    for swap in swaps:
        swap.wait_send()
    for first in range(0, CHUNKS, AG1_GROUP):
        landed(ag1, a_send, first, AG1_GROUP)

    for ch in range(CHUNKS):
        if ch % RS_GROUP == 0:
            landed(rsr, r_recv, ch, RS_GROUP)
        total = rsr[0, ch].astype(F32)
        for j in range(1, CHIPS):
            total = total + rsr[j, ch].astype(F32)
        ag2[me, ch] = (ag1[me, ch].astype(F32) + total).astype(BF16)
        if (ch + 1) % AG2_GROUP == 0:
            spread(lambda chip: ag2.at[me], ag2, n_send, n_recv, ch + 1 - AG2_GROUP, AG2_GROUP)

    for ch in range(CHUNKS):
        pltpu.make_async_copy(xs.at[1, ch], xs.at[1, ch], x_recv.at[ch]).wait()
        x = xs[1, ch]
        own_units(CHUNKS + ch, nt(wct[:LANES], x) + ecb[CHUNKS + ch, 0])
        xt[:, (CHUNKS + ch) * LANES : (CHUNKS + ch + 1) * LANES] = x.T

    for ch in range(CHUNKS):
        pltpu.make_async_copy(xs.at[0, ch], xs.at[0, ch], x_send.at[ch]).wait()
    for first in range(0, CHUNKS, RS_GROUP):
        landed(rss, r_send, first, RS_GROUP)

    for ch in range(CHUNKS):
        if ch % AG2_GROUP == 0:
            landed(ag2, n_recv, ch, AG2_GROUP)
        x = jnp.concatenate([unfold(ag2[j, ch].astype(F32)) for j in range(CHIPS)], axis=0).astype(BF16)
        pre = nt(wct[...], x)
        pre0 = pre[:LANES] + ecn[ch, 0]
        pre1 = pre[LANES:256] + ecn[ch, 1]
        weighted = pre0 * sigmoid(pre0) * heads[0] + pre1 * sigmoid(pre1) * heads[1]
        value = jnp.sum(weighted, axis=0, keepdims=True)
        ph6[me, ch : ch + 1] = discount * value + jnp.where(lane // 8 == me, pre[256:257], 0.0)
    ph6[me, 3:6] = qv[0:3]

    def share(other, step):
        return pltpu.make_async_remote_copy(
            src_ref=ph6.at[me],
            dst_ref=ph6.at[other * CHIPS + me],
            send_sem=s_send.at[0],
            recv_sem=s_recv.at[0],
            device_id=peer(step, other)[1],
            device_id_type=MESH,
        )

    for other, step in PLANE_ORDER:
        share(other, step).start()
    for first in range(0, CHUNKS, AG2_GROUP):
        landed(ag2, n_send, first, AG2_GROUP)
    slots = ph6.at[pl.ds(0, 31)]
    pltpu.make_async_copy(slots, slots, s_recv.at[0]).wait()
    halves = []
    for half in range(2):
        sums = ph6[half * CHIPS]
        for j in range(1, CHIPS):
            sums = sums + ph6[half * CHIPS + j]
        halves.append(sums)
    zb[zi] = jnp.concatenate([halves[0][:3], halves[1][:3], jnp.zeros((2, LANES), F32)], axis=0)
    for step in Z_ORDER:
        pltpu.make_async_remote_copy(
            src_ref=zb.at[zi],
            dst_ref=zb.at[zi],
            send_sem=s_send.at[1],
            recv_sem=s_recv.at[1],
            device_id=(dp, along[step]),
            device_id_type=MESH,
        ).start()
    slots = ph6.at[pl.ds(0, 31)]
    pltpu.make_async_copy(slots, slots, s_send.at[0]).wait()
    slots = zb.at[pl.ds(0, MEMBERS - 1)]
    pltpu.make_async_copy(slots, slots, s_recv.at[1]).wait()
    total = zb[0]
    square = total * total
    for m in range(1, MEMBERS):
        one = zb[m]
        total = total + one
        square = square + one * one
    mean = total / MEMBERS
    spread = square / MEMBERS - mean * mean
    target = mean - penalty_weight * jnp.sqrt(spread + 1.0)

    turned = pltpu.roll(target, (LANES - 8 * me) % LANES, 1)
    line = turned[0:1]
    for ch in range(1, CHUNKS):
        line = jnp.where(lane // 8 == ch, pltpu.roll(turned, 8 * ch, 1)[ch : ch + 1], line)
    tgt_ref[...] = line[:, :24]

    head_sum = jnp.zeros((LANES, LANES), F32)
    for half in range(2):
        for ch in range(CHUNKS):
            slot = half * CHUNKS + ch
            scaled = cnt[slot][:1] * (halves[half][3 + ch : 4 + ch] - target[slot : slot + 1])
            head_sum = head_sum + scaled * at[slot]
            bt[:, slot * LANES : (slot + 1) * LANES] = (scaled * gt[slot]).astype(BF16)
    back = bt[...]
    gin_ref[...] = nt(xt[...], back)
    hots = jnp.concatenate([hot_t(slot, 0) for slot in range(2 * CHUNKS)], axis=1)
    gemb_ref[...] = nt(hots, back).reshape(ACTS, 1, LANES)
    ghead_ref[...] = jnp.sum(head_sum.T, axis=0, keepdims=True)

    slots = zb.at[pl.ds(0, MEMBERS - 1)]
    pltpu.make_async_copy(slots, slots, s_send.at[1]).wait()


def finish(gin_ref, gemb_ref, ghead_ref, tgt_ref, gin_out, gemb_out, ghead_out, tgt_out, sem):
    copies = [
        pltpu.make_async_copy(src, dst, sem.at[i])
        for i, (src, dst) in enumerate(
            [(gin_ref, gin_out), (gemb_ref.at[pl.ds(0, 18)], gemb_out), (ghead_ref, ghead_out), (tgt_ref, tgt_out)]
        )
    ]
    for copy in copies:
        copy.start()
    for copy in copies:
        copy.wait()


def local(
    logged,
    row_ids,
    actions,
    next_actions,
    boot,
    dyn_in,
    dyn_embed,
    dyn_out,
    reward_head,
    critic_in,
    critic_embed,
    critic_head,
):
    vmem = pl.BlockSpec(memory_space=pltpu.VMEM)
    hbm = pl.BlockSpec(memory_space=pltpu.HBM)
    dma = pltpu.SemaphoreType.DMA
    blocks = (CHIPS, CHUNKS, 16, HALF)
    def shapes(rows):
        return tuple(
            jax.ShapeDtypeStruct(shape, F32) for shape in ((WIDTH, LANES), (rows, 1, LANES), (1, LANES), (1, 24))
        )

    results = pl.pallas_call(
        kernel,
        out_shape=shapes(ACTS),
        in_specs=[hbm] * 12,
        out_specs=(vmem,) * 4,
        scratch_shapes=[
            pltpu.VMEM((1, 24), jnp.int32),
            pltpu.VMEM((768,), jnp.int32),
            pltpu.VMEM((768,), jnp.int32),
            pltpu.VMEM((1, 768), jnp.int32),
            pltpu.VMEM((1, WIDTH), BF16),
            pltpu.VMEM((1, LANES), BF16),
            pltpu.VMEM((18, 256), BF16),
            pltpu.VMEM((18, LANES), BF16),
            pltpu.VMEM((256, WIDTH), BF16),
            pltpu.VMEM((2, WIDTH, 256), BF16),
            pltpu.VMEM((2, 256, WIDTH), BF16),
            pltpu.VMEM((2, WIDTH, LANES), BF16),
            pltpu.VMEM((2, ACTS, 256), BF16),
            pltpu.VMEM((2, ACTS, LANES), BF16),
            pltpu.VMEM((2, 8, LANES), F32),
            pltpu.VMEM(blocks, BF16),
            pltpu.VMEM((2, CHUNKS, LANES, WIDTH), BF16),
            pltpu.VMEM((CHUNKS, 2, LANES, 256), F32),
            pltpu.VMEM(blocks, BF16),
            pltpu.VMEM(blocks, BF16),
            pltpu.VMEM(blocks, BF16),
            pltpu.VMEM((272, WIDTH), BF16),
            pltpu.VMEM((CHUNKS, 2, LANES, LANES), F32),
            pltpu.VMEM((2 * CHUNKS, 2, LANES, LANES), F32),
            pltpu.VMEM((2 * CHUNKS, LANES, LANES), F32),
            pltpu.VMEM((2 * CHUNKS, LANES, LANES), F32),
            pltpu.VMEM((WIDTH, 768), BF16),
            pltpu.VMEM((LANES, 768), BF16),
            pltpu.VMEM((2 * CHUNKS, 8, LANES), F32),
            pltpu.VMEM((2 * CHUNKS, 8, LANES), F32),
            pltpu.VMEM((8, LANES), F32),
            pltpu.VMEM((2 * CHIPS, 8, LANES), F32),
            pltpu.VMEM((MEMBERS, 8, LANES), F32),
            dma((12,)),
            dma((6,)),
            dma((6,)),
            dma((CHUNKS,)),
            dma((CHUNKS,)),
            dma((CHUNKS,)),
            dma((CHUNKS,)),
            dma((CHUNKS,)),
            dma((CHUNKS,)),
            dma((CHUNKS,)),
            dma((CHUNKS,)),
            dma((2,)),
            dma((2,)),
        ],
        compiler_params=pltpu.CompilerParams(
            collective_id=0, has_side_effects=True, vmem_limit_bytes=60 * 2**20
        ),
        name="rollout",
    )(
        row_ids[None],
        actions,
        next_actions,
        boot,
        reward_head,
        critic_head,
        dyn_embed[0],
        critic_embed[0],
        logged,
        dyn_in[0],
        dyn_out[0],
        critic_in[0],
    )
    grad_in, grad_embed, grad_head, target = pl.pallas_call(
        finish,
        out_shape=shapes(18),
        in_specs=[vmem] * 4,
        out_specs=(hbm,) * 4,
        scratch_shapes=[dma((4,))],
        compiler_params=pltpu.CompilerParams(vmem_limit_bytes=60 * 2**20),
        name="finish",
    )(*results)
    return grad_in[None], grad_embed.transpose(1, 0, 2), grad_head, target[0]


def solution(mesh):
    return jax.shard_map(
        local,
        mesh=mesh,
        in_specs=(
            P("dp", None),
            P("dp"),
            P(),
            P(),
            P("mp", None),
            P("mp", None, "dp"),
            P("mp", None, "dp"),
            P("mp", "dp", None),
            P("mp", None),
            P("mp", None, "dp"),
            P("mp", None, "dp"),
            P("mp", "dp"),
        ),
        out_specs=(P("mp", None, "dp"), P("mp", None, "dp"), P("mp", "dp"), P("dp")),
        check_vma=False,
    )
```
